32 devices in a mesh: dp: 8 (over z, x), tensor: 4 (over y, core).
Axes of the slice: x: 2, y: 2, z: 4, core: 2. Of those that a mesh axis runs over, the one named last changes fastest.
Arguments:
- activations: bfloat16 [4096, 4096], P('dp', 'tensor'), may hold values from -6 to 6
- base_weight: bfloat16 [4096, 4096], P('tensor'), may hold values from -8.4375 to 8.4375
- adapter_in: float32 [4096, 64], P('tensor'), may hold values from -0.09375 to 0.09375
- adapter_out: float32 [64, 4096], replicated, may hold values from -0.75 to 0.75
- magnitude: float32 [4096], replicated, may hold values from 0.5 to 2
- cotangent: bfloat16 [4096, 4096], P(('dp', 'tensor')), may hold values from -1.5 to 1.5
Outputs:
- output: bfloat16 [4096, 4096], P(('dp', 'tensor'))
- grad_act: bfloat16 [4096, 4096], P('dp', 'tensor')
- grad_in: float32 [4096, 64], P('tensor')
- grad_out: float32 [64, 4096], replicated
- grad_mag: float32 [4096], replicated
The draws below stay inside these ranges and needn't reach their ends.
All inputs are finite; a program needn't handle non-finite values.
Results may differ from the reference program's by a relative error of at most 0.0057.
Values may be sent and summed in bfloat16 or wider, within the bound.
A program may use at most 128 MiB of HBM per device.

```python
import math
import jax
import jax.numpy as jnp
from jax import lax

IN = 4096
OUT = 4096
R = 64
TOKENS = 4096


def draw_base_weight(key, part):
    keys = jax.random.split(jax.random.fold_in(key, 11), 3)
    noise = jnp.clip(jax.random.normal(keys[0], (IN, OUT), jnp.float32), -6.0, 6.0)
    ramp = jnp.exp(jnp.log(3.0) * jnp.arange(IN, dtype=jnp.float32) / IN)[:, None]
    row_scale = jnp.exp(jax.random.uniform(keys[1], (IN, 1), jnp.float32) * jnp.log(10.0)) * ramp
    col_scale = jnp.exp(jax.random.uniform(keys[2], (1, OUT), jnp.float32) * jnp.log(10.0))
    return (noise * row_scale * col_scale / (10.0 * jnp.sqrt(jnp.float32(IN)))).astype(jnp.bfloat16)


def block_levels(rng, extent, cuts, low, high):
    loudness, own = 1.0, jax.random.fold_in(rng, 6)
    for axis_at, blocks in cuts:
        draws = jnp.exp(jax.random.uniform(jax.random.fold_in(own, axis_at), (blocks,), jnp.float32, low / len(cuts), high / len(cuts)))
        loudness = loudness * jnp.repeat(draws, extent[axis_at] // blocks).reshape([-1 if axis == axis_at else 1 for axis in range(len(extent))])
    return loudness


def gaussian(rng, shape, width, limit, cuts=(), kind=jnp.bfloat16):
    level = block_levels(rng, shape, cuts, -0.22, 0.18) if cuts else 1.0
    values = jax.random.normal(rng, shape, jnp.float32) * width * level
    return jnp.minimum(jnp.maximum(values, -limit), limit).astype(kind)


def setup_inputs(seed: int = 0) -> dict:
    key_list = jax.random.split(jax.random.key(seed), 7)
    return {
        "activations": gaussian(key_list[0], (TOKENS, IN), 1.0, 6.0, ((0, 8), (1, 4))),
        "base_weight": draw_base_weight(jax.random.fold_in(key_list[6], 71), 0),
        "adapter_in": gaussian(key_list[2], (IN, R), IN ** -0.5, 0.09375, ((0, 4),), jnp.float32),
        "adapter_out": gaussian(key_list[3], (R, OUT), R ** -0.5, 0.75, (), jnp.float32),
        "magnitude": jnp.clip(jnp.exp(jax.random.uniform(key_list[4], (OUT,), jnp.float32, math.log(0.5), math.log(2.0))), 0.5, 2.0),
        "cotangent": gaussian(key_list[5], (TOKENS, OUT), 0.25, 1.5, ((0, 32),)),
    }


epsilon = 1e-06

def reference(activations, base_weight, adapter_in, adapter_out, magnitude, cotangent):
    highest = lax.Precision.HIGHEST
    merged = base_weight.astype(jnp.float32) + jnp.dot(adapter_in, adapter_out, precision=highest)
    col_norm = jnp.sqrt(lax.optimization_barrier(jnp.sum(merged * merged, axis=0)) + epsilon)
    col_scale = magnitude / col_norm
    merged_low = merged.astype(jnp.bfloat16)
    summed = jnp.dot(activations, merged_low, preferred_element_type=jnp.float32)
    output = (summed * col_scale).astype(jnp.bfloat16)
    cot_float = cotangent.astype(jnp.float32)
    grad_scaled = (cot_float * col_scale).astype(jnp.bfloat16)
    grad_act = lax.dot_general(grad_scaled, merged_low, (((1,), (1,)), ((), ())), preferred_element_type=jnp.float32).astype(jnp.bfloat16)
    grad_mag = lax.optimization_barrier(jnp.sum(cot_float * summed, axis=0)) / col_norm
    norm_coeff = -grad_mag * magnitude / (col_norm * col_norm)
    grad_dir = lax.dot_general(activations, grad_scaled, (((0,), (0,)), ((), ())), preferred_element_type=jnp.float32)
    grad_dir = grad_dir + merged * norm_coeff
    grad_in = jnp.dot(grad_dir, adapter_out.T, precision=highest)
    grad_out = jnp.dot(adapter_in.T, grad_dir, precision=highest)
    return (output, grad_act, grad_in, grad_out, grad_mag)
```

```python
import jax
import jax.numpy as jnp
from jax import lax
from jax.sharding import PartitionSpec as P

epsilon = 1e-06
low = jnp.bfloat16
full = jnp.float32


def mm(a, b, ca, cb):
    return lax.dot_general(a, b, (((ca,), (cb,)), ((), ())), preferred_element_type=full)


def two_parts(x):
    high = lax.reduce_precision(x, 8, 7)
    return high.astype(low), (x - high).astype(low)


def bits_of(size):
    bits = [1 << k for k in range(size.bit_length() - 1)]
    assert 1 << len(bits) == size
    return bits


def swap(x, axis, size, bit):
    return lax.ppermute(x, axis, [(i, i ^ bit) for i in range(size)])


def total(x, axis, size):
    for bit in bits_of(size):
        x = x + swap(x, axis, size, bit)
    return x


def scatter_columns(x, axis, size):
    me = lax.axis_index(axis)
    for bit in bits_of(size):
        half = x.shape[1] // 2
        upper = (me & bit) != 0
        left, right = x[:, :half], x[:, half:]
        x = jnp.where(upper, right, left) + swap(jnp.where(upper, left, right), axis, size, bit)
    return x


def gather_columns(x, axis, size):
    me = lax.axis_index(axis)
    for bit in reversed(bits_of(size)):
        upper = (me & bit) != 0
        other = swap(x, axis, size, bit)
        x = jnp.concatenate([jnp.where(upper, other, x), jnp.where(upper, x, other)], axis=1)
    return x


def shards(dp, tp, activations, base_weight, adapter_in, adapter_out, magnitude, cotangent):
    me = lax.axis_index("tensor")
    bits = bits_of(tp)
    order = [0]
    for bit in reversed(bits):
        order = order + [k ^ bit for k in order]
    place = [order.index(k) for k in range(tp)]
    rows = cotangent.shape[0]

    cot = cotangent
    for bit in reversed(bits):
        cot = jnp.concatenate([cot, swap(cot, "tensor", tp, bit)], axis=0)

    b_high, b_low = two_parts(adapter_in)
    a_high, a_low = two_parts(adapter_out)
    lowrank = mm(
        jnp.concatenate([b_high, b_high, b_low], axis=1),
        jnp.concatenate([a_high, a_low, a_high], axis=0),
        1,
        0,
    )
    merged = base_weight.astype(full) + lowrank
    merged_low = merged.astype(low)
    square_sum = total(jnp.sum(merged * merged, axis=0)[None, :], "tensor", tp)
    col_norm = jnp.sqrt(square_sum + epsilon)
    col_scale = magnitude[None, :] / col_norm

    act = jnp.concatenate(
        [lax.dynamic_slice_in_dim(activations, (me ^ k) * rows, rows, 0) for k in order], axis=0
    )
    half = act.shape[0] // 2
    sent = mm(act[half:], merged_low, 1, 0).astype(low)
    kept = mm(act[:half], merged_low, 1, 0)
    slope = (
        jnp.sum(cot[:half].astype(full) * kept, axis=0)
        + jnp.sum(cot[half:].astype(full) * sent.astype(full), axis=0)
    )[None, :]
    summed = kept + swap(sent, "tensor", tp, bits[0]).astype(full)
    for bit in bits[1:]:
        half = summed.shape[0] // 2
        summed = summed[:half] + swap(summed[half:].astype(low), "tensor", tp, bit).astype(full)
    output = (summed * col_scale).astype(low)

    grad_scaled = (cot.astype(full) * col_scale).astype(low)
    act_rel = mm(grad_scaled, merged_low, 1, 1).astype(low)
    places = jnp.asarray(place, jnp.int32)
    grad_act = jnp.concatenate(
        [lax.dynamic_slice_in_dim(act_rel, places[me ^ k] * rows, rows, 0) for k in range(tp)], axis=0
    )

    rank = adapter_in.shape[1]
    fold = lambda x: x[:rank] + x[rank:]
    b_both = jnp.concatenate([b_high, b_low], axis=1)
    a_both = jnp.concatenate([a_high, a_low], axis=0)
    down = fold(mm(b_both, act, 0, 1))
    up = fold(mm(a_both, grad_scaled, 1, 1))
    own_dir = fold(mm(b_both, merged_low, 0, 0))
    out_part = fold(mm(jnp.concatenate(two_parts(down), axis=0), grad_scaled, 1, 0))
    in_part = fold(mm(jnp.concatenate(two_parts(up), axis=0), act, 1, 0))

    slope_replica = total(slope, "tensor", tp)
    norm_coeff = -slope_replica * magnitude[None, :] / (col_norm * col_norm * col_norm)
    out_part = out_part + norm_coeff * own_dir
    in_part = in_part + fold(
        mm(jnp.concatenate(two_parts(adapter_out * norm_coeff), axis=0), merged_low, 1, 1)
    )

    columns = scatter_columns(jnp.concatenate([out_part, slope], axis=0), "tensor", tp)
    stack = jnp.concatenate([in_part, columns], axis=0)
    stack = gather_columns(scatter_columns(stack, "dp", dp), "dp", dp)
    grad_in = stack[:rank].T
    columns = gather_columns(stack[rank:], "tensor", tp)
    grad_out = columns[:rank]
    grad_mag = (columns[rank:] / col_norm)[0]
    return (output, grad_act, grad_in, grad_out, grad_mag)


def solution(mesh):
    dp, tp = mesh.shape["dp"], mesh.shape["tensor"]
    in_specs = (
        P("dp", "tensor"),
        P("tensor", None),
        P("tensor", None),
        P(),
        P(),
        P(("dp", "tensor"), None),
    )
    out_specs = (P(("dp", "tensor"), None), P("dp", "tensor"), P("tensor", None), P(), P())

    def run(*args):
        return shards(dp, tp, *args)

    return jax.shard_map(run, mesh=mesh, in_specs=in_specs, out_specs=out_specs, check_vma=False)
```

```python
import functools

import jax
import jax.numpy as jnp
from jax import lax
from jax.experimental import pallas as pl
from jax.experimental.pallas import tpu as pltpu
from jax.sharding import PartitionSpec as P

epsilon = 1e-06
low = jnp.bfloat16
full = jnp.float32


def mm(a, b, ca, cb):
    return lax.dot_general(a, b, (((ca,), (cb,)), ((), ())), preferred_element_type=full)


def tie(*arrays):
    return lax.optimization_barrier(arrays)


def two_parts(x):
    high = lax.reduce_precision(x, 8, 7)
    return high.astype(low), (x - high).astype(low)


def bits_of(size):
    bits = [1 << k for k in range(size.bit_length() - 1)]
    assert 1 << len(bits) == size
    return bits


def swap(x, axis, size, bit):
    return lax.ppermute(x, axis, [(i, i ^ bit) for i in range(size)])


def total(x, axis, size):
    for bit in bits_of(size):
        x = x + swap(x, axis, size, bit)
    return x


def greet(axis, size):
    me = lax.axis_index(axis)
    barrier = pltpu.get_barrier_semaphore()
    for k in range(1, size):
        pl.semaphore_signal(
            barrier,
            inc=1,
            device_id={axis: lax.rem(me + k, size)},
            device_id_type=pl.DeviceIdType.MESH,
        )
    pl.semaphore_wait(barrier, size - 1)
    return me


def send_all(axis, size, me, source, slots, sends, recvs):
    copies = []
    for k in range(1, size):
        peer = lax.rem(me + k, size)
        copy = pltpu.make_async_remote_copy(
            src_ref=source(peer),
            dst_ref=slots.at[me],
            send_sem=sends.at[k - 1],
            recv_sem=recvs.at[k - 1],
            device_id={axis: peer},
            device_id_type=pl.DeviceIdType.MESH,
        )
        copy.start()
        copies.append(copy)
    return copies


def exchange_kernel(axis, size, scatter, gather, x_ref, o_ref, *scratch):
    me = greet(axis, size)
    mine = x_ref
    if scatter:
        slots, sends, recvs, *scratch = scratch
        copies = send_all(axis, size, me, lambda p: x_ref.at[p], slots, sends, recvs)
        slots[me] = x_ref[me]
        for copy in copies:
            copy.wait()
        sums = slots[0].astype(full)
        for k in range(1, size):
            sums = sums + slots[k].astype(full)
        if not gather:
            o_ref[...] = sums
            return
        mine, *scratch = scratch
        mine[...] = sums.astype(low)
    slots, sends, recvs = scratch
    copies = send_all(axis, size, me, lambda p: mine, slots, sends, recvs)
    slots[me] = mine[...]
    for copy in copies:
        copy.wait()
    o_ref[...] = slots[...].astype(full)


def exchange(x, axis, size, scatter, gather, ident):
    block = x.shape[1:] if scatter else x.shape
    group = [
        pltpu.VMEM((size, *block), low),
        pltpu.SemaphoreType.DMA((size - 1,)),
        pltpu.SemaphoreType.DMA((size - 1,)),
    ]
    scratch = group if scatter else []
    if scatter and gather:
        scratch = scratch + [pltpu.VMEM(block, low)]
    if gather:
        scratch = scratch + group
    return pl.pallas_call(
        functools.partial(exchange_kernel, axis, size, scatter, gather),
        out_shape=jax.ShapeDtypeStruct((size, *block) if gather else block, full),
        in_specs=[pl.BlockSpec(memory_space=pltpu.VMEM)],
        out_specs=pl.BlockSpec(memory_space=pltpu.VMEM),
        scratch_shapes=scratch,
        compiler_params=pltpu.CompilerParams(
            collective_id=ident, has_side_effects=True, vmem_limit_bytes=24 * 2**20
        ),
    )(x)


def shards(dp, tp, activations, base_weight, adapter_in, adapter_out, magnitude, cotangent):
    me = lax.axis_index("tensor")
    bits = bits_of(tp)
    order = [0]
    for bit in reversed(bits):
        order = order + [k ^ bit for k in order]
    place = [order.index(k) for k in range(tp)]
    rows = cotangent.shape[0]

    quarter = rows // 4
    quarters = []
    for i in range(4):
        part = cotangent[i * quarter : (i + 1) * quarter]
        for bit in reversed(bits[1:]):
            part = jnp.concatenate([part, swap(part, "tensor", tp, bit)], axis=0)
        quarters.append(part)

    b_high, b_low = two_parts(adapter_in)
    a_high, a_low = two_parts(adapter_out)
    lowrank = mm(
        jnp.concatenate([b_high, b_high, b_low], axis=1),
        jnp.concatenate([a_high, a_low, a_high], axis=0),
        1,
        0,
    )
    merged = base_weight.astype(full) + lowrank
    merged_low, quarters[0] = tie(merged.astype(low), quarters[0])
    square_sum = total(jnp.sum(merged * merged, axis=0)[None, :], "tensor", tp)
    col_norm = jnp.sqrt(square_sum + epsilon)
    col_scale = magnitude[None, :] / col_norm

    act = jnp.concatenate(
        [lax.dynamic_slice_in_dim(activations, (me ^ k) * rows, rows, 0) for k in order], axis=0
    )
    half = act.shape[0] // 2
    sent = mm(act[half:], merged_low, 1, 0).astype(low)
    merged_low, sent, quarters[1] = tie(merged_low, sent, quarters[1])
    kept = mm(act[:half], merged_low, 1, 0)
    kept, quarters[2] = tie(kept, quarters[2])
    summed = kept + swap(sent, "tensor", tp, bits[0]).astype(full)
    for bit in bits[1:-1]:
        half = summed.shape[0] // 2
        summed = summed[:half] + swap(summed[half:].astype(low), "tensor", tp, bit).astype(full)
    passed, own = summed[rows:].astype(low), summed[:rows]
    passed, own, quarters[3] = tie(passed, own, quarters[3])
    arrived = [
        swap(passed[i * quarter : (i + 1) * quarter], "tensor", tp, bits[-1]) for i in range(4)
    ]
    cot = jnp.concatenate([part.reshape(-1, quarter, part.shape[1]) for part in quarters], axis=1)
    cot = cot.reshape(-1, cot.shape[2])
    cot = jnp.concatenate([cot, swap(cot, "tensor", tp, bits[0])], axis=0)
    half = kept.shape[0]
    slope = (
        jnp.sum(cot[:half].astype(full) * kept, axis=0)
        + jnp.sum(cot[half:].astype(full) * sent.astype(full), axis=0)
    )[None, :]
    slope, cot, arrived[0] = tie(slope, cot, arrived[0])
    grad_scaled, arrived[1] = tie((cot.astype(full) * col_scale).astype(low), arrived[1])
    act_rel = mm(grad_scaled, merged_low, 1, 1).astype(low)
    act_rel, grad_scaled, arrived[2] = tie(act_rel, grad_scaled, arrived[2])
    places = jnp.asarray(place, jnp.int32)
    grad_act = jnp.concatenate(
        [lax.dynamic_slice_in_dim(act_rel, places[me ^ k] * rows, rows, 0) for k in range(tp)], axis=0
    )

    rank = adapter_in.shape[1]
    fold = lambda x: x[:rank] + x[rank:]
    b_both = jnp.concatenate([b_high, b_low], axis=1)
    a_both = jnp.concatenate([a_high, a_low], axis=0)
    down = fold(mm(b_both, act, 0, 1))
    up = fold(mm(a_both, grad_scaled, 1, 1))
    own_dir = fold(mm(b_both, merged_low, 0, 0))
    out_part = fold(mm(jnp.concatenate(two_parts(down), axis=0), grad_scaled, 1, 0))
    in_part = fold(mm(jnp.concatenate(two_parts(up), axis=0), act, 1, 0))

    slope_replica = total(slope, "tensor", tp)
    norm_coeff = -slope_replica * magnitude[None, :] / (col_norm * col_norm * col_norm)
    out_part = out_part + norm_coeff * own_dir
    out_part, in_part, norm_coeff, arrived[3] = tie(out_part, in_part, norm_coeff, arrived[3])
    in_part = in_part + fold(
        mm(jnp.concatenate(two_parts(adapter_out * norm_coeff), axis=0), merged_low, 1, 1)
    )

    out_part, in_part, grad_act = tie(out_part, in_part, grad_act)
    output = ((own + jnp.concatenate(arrived, axis=0).astype(full)) * col_scale).astype(low)
    wide = out_part.shape[1]
    block = wide // tp
    padded = jnp.concatenate([out_part, slope, jnp.zeros((15, wide), full)], axis=0).astype(low)
    extra = padded.shape[0]
    columns = exchange(
        padded.reshape(extra, tp, block).transpose(1, 0, 2), "tensor", tp, True, False, 0
    )
    stack = jnp.concatenate([in_part, columns], axis=0).astype(low)
    high = stack.shape[0]
    unit = dp * 16 * 128
    count = -(-stack.size // unit) * unit
    flat = stack.reshape(high, block // 128, 128).transpose(1, 0, 2).reshape(-1, 128)
    flat = jnp.pad(flat, ((0, count // 128 - flat.shape[0]), (0, 0)))
    flat = exchange(flat.reshape(dp, -1, 128), "dp", dp, True, True, 1).reshape(-1, 128)
    flat = flat[: stack.size // 128].reshape(block // 128, high, 128)
    stack = flat.transpose(1, 0, 2).reshape(high, block)
    grad_in = stack[:rank].T
    columns = exchange(stack[rank:].astype(low), "tensor", tp, False, True, 2)
    columns = columns.transpose(1, 0, 2).reshape(extra, wide)
    grad_out = columns[:rank]
    grad_mag = (columns[rank : rank + 1] / col_norm)[0]
    return (output, grad_act, grad_in, grad_out, grad_mag)


def solution(mesh):
    dp, tp = mesh.shape["dp"], mesh.shape["tensor"]
    in_specs = (
        P("dp", "tensor"),
        P("tensor", None),
        P("tensor", None),
        P(),
        P(),
        P(("dp", "tensor"), None),
    )
    out_specs = (P(("dp", "tensor"), None), P("dp", "tensor"), P("tensor", None), P(), P())

    def run(*args):
        return shards(dp, tp, *args)

    return jax.shard_map(run, mesh=mesh, in_specs=in_specs, out_specs=out_specs, check_vma=False)
```

```python
import functools

import jax
import jax.numpy as jnp
from jax import lax
from jax.experimental import pallas as pl
from jax.experimental.pallas import tpu as pltpu
from jax.sharding import PartitionSpec as P

epsilon = 1e-06
low = jnp.bfloat16
full = jnp.float32


def mm(a, b, ca, cb):
    return lax.dot_general(a, b, (((ca,), (cb,)), ((), ())), preferred_element_type=full)


def tie(*arrays):
    return lax.optimization_barrier(arrays)


def two_parts(x):
    high = lax.reduce_precision(x, 8, 7)
    return high.astype(low), (x - high).astype(low)


def bits_of(size):
    bits = [1 << k for k in range(size.bit_length() - 1)]
    assert 1 << len(bits) == size
    return bits


def swap(x, axis, size, bit):
    return lax.ppermute(x, axis, [(i, i ^ bit) for i in range(size)])


def total(x, axis, size):
    for bit in bits_of(size):
        x = x + swap(x, axis, size, bit)
    return x


def greet(axis, size):
    me = lax.axis_index(axis)
    barrier = pltpu.get_barrier_semaphore()
    for k in range(1, size):
        pl.semaphore_signal(
            barrier,
            inc=1,
            device_id={axis: lax.rem(me + k, size)},
            device_id_type=pl.DeviceIdType.MESH,
        )
    pl.semaphore_wait(barrier, size - 1)
    return me


def send_all(axis, size, me, source, slots, sends, recvs):
    copies = []
    for k in range(1, size):
        peer = lax.rem(me + k, size)
        copy = pltpu.make_async_remote_copy(
            src_ref=source(peer),
            dst_ref=slots.at[me],
            send_sem=sends.at[k - 1],
            recv_sem=recvs.at[k - 1],
            device_id={axis: peer},
            device_id_type=pl.DeviceIdType.MESH,
        )
        copy.start()
        copies.append(copy)
    return copies


def exchange_kernel(axis, size, scatter, gather, x_ref, o_ref, *scratch):
    me = greet(axis, size)
    mine = x_ref
    if scatter:
        slots, sends, recvs, *scratch = scratch
        copies = send_all(axis, size, me, lambda p: x_ref.at[p], slots, sends, recvs)
        slots[me] = x_ref[me]
        for copy in copies:
            copy.wait()
        sums = slots[0].astype(full)
        for k in range(1, size):
            sums = sums + slots[k].astype(full)
        if not gather:
            o_ref[...] = sums
            return
        mine, *scratch = scratch
        mine[...] = sums.astype(low)
    slots, sends, recvs = scratch
    copies = send_all(axis, size, me, lambda p: mine, slots, sends, recvs)
    slots[me] = mine[...]
    for copy in copies:
        copy.wait()
    o_ref[...] = slots[...].astype(full)


def exchange(x, axis, size, scatter, gather, ident):
    block = x.shape[1:] if scatter else x.shape
    group = [
        pltpu.VMEM((size, *block), low),
        pltpu.SemaphoreType.DMA((size - 1,)),
        pltpu.SemaphoreType.DMA((size - 1,)),
    ]
    scratch = group if scatter else []
    if scatter and gather:
        scratch = scratch + [pltpu.VMEM(block, low)]
    if gather:
        scratch = scratch + group
    return pl.pallas_call(
        functools.partial(exchange_kernel, axis, size, scatter, gather),
        out_shape=jax.ShapeDtypeStruct((size, *block) if gather else block, full),
        in_specs=[pl.BlockSpec(memory_space=pltpu.VMEM)],
        out_specs=pl.BlockSpec(memory_space=pltpu.VMEM),
        scratch_shapes=scratch,
        compiler_params=pltpu.CompilerParams(
            collective_id=ident, has_side_effects=True, vmem_limit_bytes=24 * 2**20
        ),
    )(x)


def shards(dp, tp, activations, base_weight, adapter_in, adapter_out, magnitude, cotangent):
    me = lax.axis_index("tensor")
    bits = bits_of(tp)
    order = [0]
    for bit in reversed(bits):
        order = order + [k ^ bit for k in order]
    place = [order.index(k) for k in range(tp)]
    rows = cotangent.shape[0]

    quarter = rows // 4
    halves = []
    for i in range(2):
        part = cotangent[i * 2 * quarter : (i + 1) * 2 * quarter]
        for bit in reversed(bits[1:]):
            part = jnp.concatenate([part, swap(part, "tensor", tp, bit)], axis=0)
        halves.append(part)

    b_high, b_low = two_parts(adapter_in)
    a_high, a_low = two_parts(adapter_out)
    lowrank = mm(
        jnp.concatenate([b_high, b_high, b_low], axis=1),
        jnp.concatenate([a_high, a_low, a_high], axis=0),
        1,
        0,
    )
    merged = base_weight.astype(full) + lowrank
    merged_low, halves[0] = tie(merged.astype(low), halves[0])
    square_sum = total(jnp.sum(merged * merged, axis=0)[None, :], "tensor", tp)

    act = jnp.concatenate(
        [lax.dynamic_slice_in_dim(activations, (me ^ k) * rows, rows, 0) for k in order], axis=0
    )
    half = act.shape[0] // 2
    sent = mm(act[half:], merged_low, 1, 0).astype(low)
    merged_low, sent, halves[1] = tie(merged_low, sent, halves[1])
    kept = mm(act[:half], merged_low, 1, 0)
    summed = kept + swap(sent, "tensor", tp, bits[0]).astype(full)
    for bit in bits[1:-1]:
        half = summed.shape[0] // 2
        summed = summed[:half] + swap(summed[half:].astype(low), "tensor", tp, bit).astype(full)
    passed, own = summed[rows:].astype(low), summed[:rows]
    passed, own, square_sum = tie(passed, own, square_sum)
    col_norm = jnp.sqrt(square_sum + epsilon)
    col_scale = magnitude[None, :] / col_norm
    arrived = [swap(part, "tensor", tp, bits[-1]) for part in (passed[:quarter], passed[quarter:])]
    cot = jnp.concatenate([part.reshape(-1, 2 * quarter, part.shape[1]) for part in halves], axis=1)
    cot = cot.reshape(-1, cot.shape[2])
    cot = jnp.concatenate([cot, swap(cot, "tensor", tp, bits[0])], axis=0)
    cot, arrived[0] = tie(cot, arrived[0])
    half = kept.shape[0]
    slope = (
        jnp.sum(cot[:half].astype(full) * kept, axis=0)
        + jnp.sum(cot[half:].astype(full) * sent.astype(full), axis=0)
    )[None, :]
    grad_scaled = (cot.astype(full) * col_scale).astype(low)
    act_rel = mm(grad_scaled, merged_low, 1, 1).astype(low)
    act_rel, grad_scaled, arrived[1] = tie(act_rel, grad_scaled, arrived[1])
    places = jnp.asarray(place, jnp.int32)
    grad_act = jnp.concatenate(
        [lax.dynamic_slice_in_dim(act_rel, places[me ^ k] * rows, rows, 0) for k in range(tp)], axis=0
    )

    rank = adapter_in.shape[1]
    fold = lambda x: x[:rank] + x[rank:]
    b_both = jnp.concatenate([b_high, b_low], axis=1)
    a_both = jnp.concatenate([a_high, a_low], axis=0)
    down = fold(mm(b_both, act, 0, 1))
    up = fold(mm(a_both, grad_scaled, 1, 1))
    own_dir = fold(mm(b_both, merged_low, 0, 0))
    out_part = fold(mm(jnp.concatenate(two_parts(down), axis=0), grad_scaled, 1, 0))
    in_part = fold(mm(jnp.concatenate(two_parts(up), axis=0), act, 1, 0))

    slope_replica = total(slope, "tensor", tp)
    norm_coeff = -slope_replica * magnitude[None, :] / (col_norm * col_norm * col_norm)
    out_part = out_part + norm_coeff * own_dir
    in_part = in_part + fold(
        mm(jnp.concatenate(two_parts(adapter_out * norm_coeff), axis=0), merged_low, 1, 1)
    )

    out_part, in_part, grad_act = tie(out_part, in_part, grad_act)
    output = ((own + jnp.concatenate(arrived, axis=0).astype(full)) * col_scale).astype(low)
    wide = out_part.shape[1]
    block = wide // tp
    padded = jnp.concatenate([out_part, slope, jnp.zeros((15, wide), full)], axis=0).astype(low)
    extra = padded.shape[0]
    columns = exchange(
        padded.reshape(extra, tp, block).transpose(1, 0, 2), "tensor", tp, True, False, 0
    )
    stack = jnp.concatenate([in_part, columns], axis=0).astype(low)
    high = stack.shape[0]
    unit = dp * 16 * 128
    count = -(-stack.size // unit) * unit
    flat = stack.reshape(high, block // 128, 128).transpose(1, 0, 2).reshape(-1, 128)
    flat = jnp.pad(flat, ((0, count // 128 - flat.shape[0]), (0, 0)))
    flat = exchange(flat.reshape(dp, -1, 128), "dp", dp, True, True, 1).reshape(-1, 128)
    flat = flat[: stack.size // 128].reshape(block // 128, high, 128)
    stack = flat.transpose(1, 0, 2).reshape(high, block)
    grad_in = stack[:rank].T
    columns = exchange(stack[rank:].astype(low), "tensor", tp, False, True, 2)
    columns = columns.transpose(1, 0, 2).reshape(extra, wide)
    grad_out = columns[:rank]
    grad_mag = (columns[rank : rank + 1] / col_norm)[0]
    return (output, grad_act, grad_in, grad_out, grad_mag)


def solution(mesh):
    dp, tp = mesh.shape["dp"], mesh.shape["tensor"]
    in_specs = (
        P("dp", "tensor"),
        P("tensor", None),
        P("tensor", None),
        P(),
        P(),
        P(("dp", "tensor"), None),
    )
    out_specs = (P(("dp", "tensor"), None), P("dp", "tensor"), P("tensor", None), P(), P())

    def run(*args):
        return shards(dp, tp, *args)

    return jax.shard_map(run, mesh=mesh, in_specs=in_specs, out_specs=out_specs, check_vma=False)
```
